32 devices in a mesh: rows: 8 (over z, x), cols: 4 (over y, core).
Axes of the slice: x: 2, y: 2, z: 4, core: 2. Of those that a mesh axis runs over, the one named last changes fastest.
Arguments:
- graph_tiles: bfloat16 [128, 17, 128, 128], P('rows'), as said below
- tile_column: int32 [128, 17], P('rows'), may hold values from 0 to 127, as said below
- tile_count: int32 [128], P('rows'), may hold values from 1 to 17, as said below
- class_label: int32 [16384], P('rows'), may hold values from 0 to 999
- confidence: float32 [16384], P('rows'), may hold values from 0.2 to 1
- class_weight: float32 [1000], P('cols'), may hold values from 0.25 to 4
Outputs:
- scores: float32 [16384, 1000], P('rows', 'cols')
- residual: float32 [16384, 1000], P('rows', 'cols')
The draws below stay inside these ranges and needn't reach their ends.
Inputs may be any that keep to these rules, and one draw needn't show every extreme that they name: `tile_column`: Block-row i's live tiles lie in distinct block-columns (i + d) mod 128 with |d| <= 8; block-row i has a live tile in block-column j exactly when block-row j has one in block-column i. `tile_count`: slots at and beyond a block-row's count are unused. `graph_tiles`: the matrix S assembled from the live tiles is symmetric: the tile of block-row i in block-column j is the transpose of the tile of block-row j in block-column i. Entries of a live tile of block-row i in block-column j lie between 0 and 1 / (128 * sqrt(tile_count[i] * tile_count[j])).
All inputs are finite; a program needn't handle non-finite values.
Results may differ from the reference program's by a relative error of at most 0.003.
Values may be sent and summed in bfloat16 or wider, within the bound.
A program may use at most 128 MiB of HBM per device.

```python
import math
import jax
import jax.numpy as jnp
import numpy as np
from jax import lax

C = 1000
B = 128
ITERS = 3
BR_DEV = 16
HALF = 8
KMAX = 17
NB = 128
NROWS = 16384


def graph_pattern(key):
    keys = jax.random.split(jax.random.fold_in(key, 101), 3)
    row_ids = jnp.arange(NB, dtype=jnp.int32)
    distance = jnp.arange(1, HALF + 1, dtype=jnp.int32)
    level = jax.random.randint(keys[0], (NB // BR_DEV,), 1, 9)
    level_rows = jnp.repeat(level, BR_DEV)
    coins = jax.random.randint(keys[1], (NB, HALF), 0, 8)
    pair_bits = coins < level_rows[:, None]
    first_row = jax.random.randint(keys[2], (), 0, NB)
    second_row = jnp.mod(first_row + NB // 2, NB)
    partner = jnp.mod(row_ids[:, None] + distance[None, :], NB)
    touch_first = (row_ids[:, None] == first_row) | (partner == first_row)
    touch_second = (row_ids[:, None] == second_row) | (partner == second_row)
    pair_bits = jnp.where(touch_first, True, pair_bits)
    pair_bits = jnp.where(touch_second, False, pair_bits)
    plus_live = pair_bits
    behind = jnp.mod(row_ids[:, None] - distance[None, :], NB)
    minus_live = pair_bits[behind, jnp.arange(HALF, dtype=jnp.int32)[None, :]]
    side_live = jnp.stack([plus_live, minus_live], axis=2).reshape(NB, 2 * HALF)
    live = jnp.concatenate([jnp.ones((NB, 1), dtype=bool), side_live], axis=1)
    offset_table = jnp.stack([distance, -distance], axis=1).reshape(2 * HALF)
    offset_table = jnp.concatenate([jnp.zeros((1,), jnp.int32), offset_table])
    counts = jnp.sum(live.astype(jnp.int32), axis=1).astype(jnp.int32)
    order = jnp.argsort(1 - live.astype(jnp.int32), axis=1, stable=True)
    live_sorted = jnp.take_along_axis(live, order, axis=1)
    offset_sorted = offset_table[order]
    columns = jnp.where(live_sorted, jnp.mod(row_ids[:, None] + offset_sorted, NB), row_ids[:, None])
    return (order, live_sorted, columns.astype(jnp.int32), counts)


def draw_graph_tiles(key, part):
    order, live_sorted, columns, counts = graph_pattern(key)
    raw = jax.random.uniform(jax.random.fold_in(key, 202), (NB, HALF + 1, B, B), jnp.float32)
    base = 1.0 - 0.5 * raw
    row_ids = jnp.arange(NB, dtype=jnp.int32)
    diagonal_tile = 0.5 * (base[:, 0] + jnp.swapaxes(base[:, 0], 1, 2))
    pieces = [diagonal_tile]
    for dist in range(1, HALF + 1):
        pieces.append(base[:, dist])
        behind = jnp.mod(row_ids - dist, NB)
        pieces.append(jnp.swapaxes(base[behind, dist], 1, 2))
    candidates = jnp.stack(pieces, axis=1)
    sorted_tiles = jnp.take_along_axis(candidates, order[:, :, None, None], axis=1)
    own_count = counts.astype(jnp.float32)[:, None]
    other_count = counts[columns].astype(jnp.float32)
    scale = 1.0 / (B * jnp.sqrt(own_count * other_count))
    scale = jnp.where(live_sorted, scale, 0.0)
    return (sorted_tiles * scale[:, :, None, None]).astype(jnp.bfloat16)


def draw_tile_column(key, part):
    order, live_sorted, columns, counts = graph_pattern(key)
    return columns


def draw_tile_count(key, part):
    order, live_sorted, columns, counts = graph_pattern(key)
    return counts


def with_ends(drawn, key, low, largest):
    shape = drawn.shape
    spot = [jax.random.randint(jax.random.fold_in(key, axis), (), 0, shape[axis]) for axis in range(len(shape))]
    drawn = drawn.at[tuple(spot)].set(low)
    longest = shape.index(max(shape))
    spot[longest] = (spot[longest] + 1) % shape[longest]
    return drawn.at[tuple(spot)].set(largest)


def shard_levels(rng, shape, cuts, low, high):
    gain, own = 1.0, jax.random.fold_in(rng, 6)
    for axis_at, shards_of in cuts:
        steps = jnp.exp(jax.random.uniform(jax.random.fold_in(own, axis_at), (shards_of,), jnp.float32, low / len(cuts), high / len(cuts)))
        gain = gain * jnp.repeat(steps, shape[axis_at] // shards_of).reshape([-1 if axis == axis_at else 1 for axis in range(len(shape))])
    return gain


def cumulative_ranks(count, slope):
    loads = [(1 << 20) // math.isqrt(rank ** slope) + 1 for rank in range(1, count + 1)]
    spread = 1 + sum(loads) // (1 << 30)
    return np.cumsum(np.array([max(1, weight // spread) for weight in loads]))


def skewed_ids(key, shape, number_of, lean):
    grid = cumulative_ranks(number_of, lean)
    lot = jax.random.randint(jax.random.fold_in(key, 1), shape, 0, int(grid[number_of - 1]))
    rank = jnp.searchsorted(jnp.asarray(grid, jnp.int32), lot, side="right")
    return jax.random.permutation(jax.random.fold_in(key, 2), number_of)[rank].astype(jnp.int32)


def setup_inputs(seed: int = 0) -> dict:
    key_list = jax.random.split(jax.random.key(seed), 7)
    return {
        "graph_tiles": draw_graph_tiles(jax.random.fold_in(key_list[6], 71), 0),
        "tile_column": draw_tile_column(jax.random.fold_in(key_list[6], 71), 0),
        "tile_count": draw_tile_count(jax.random.fold_in(key_list[6], 71), 0),
        "class_label": with_ends(skewed_ids(key_list[3], (NROWS,), C, 2), jax.random.fold_in(key_list[3], 3), 0, C - 1).astype(jnp.int32),
        "confidence": jnp.clip(jnp.exp(math.log(1.0) - 1.609438 * jax.random.uniform(key_list[4], (NROWS,), jnp.float32) ** shard_levels(key_list[4], (NROWS,), ((0, 8),), -0.2, 0.2)), 0.2, 1.0),
        "class_weight": jnp.clip(jnp.exp(math.log(4.0) - 2.7725887 * jax.random.uniform(key_list[5], (C,), jnp.float32) ** shard_levels(key_list[5], (C,), ((0, 4),), -0.2, 0.2)), 0.25, 4.0),
    }


damping = 0.99
smoothing = 0.1

def apply_operator(direction, graph_tiles, tile_column, live_slot):
    rounded = lax.optimization_barrier(direction.astype(jnp.bfloat16))
    blocks = rounded.reshape(NB, B, C)
    product_sum = jnp.zeros((NB, B, C), jnp.float32)
    for slot in range(KMAX):
        picked = blocks[tile_column[:, slot]].astype(jnp.float32)
        picked = jnp.where(live_slot[:, slot][:, None, None], picked, jnp.float32(0.0))
        tile_slot = graph_tiles[:, slot].astype(jnp.float32)
        product_sum = product_sum + jnp.einsum('rij,rjc->ric', tile_slot, picked)
    return direction - damping * product_sum.reshape(NROWS, C)

def reference(graph_tiles, tile_column, tile_count, class_label, confidence, class_weight):
    live_slot = jnp.arange(KMAX, dtype=jnp.int32)[None, :] < tile_count[:, None]
    onehot = (class_label[:, None] == jnp.arange(C, dtype=jnp.int32)[None, :]).astype(jnp.float32)
    prior_labels = confidence[:, None] * class_weight[None, :] * ((1.0 - smoothing) * onehot + smoothing / C)
    solution = jnp.zeros_like(prior_labels)
    residual = prior_labels
    direction = prior_labels
    norm_now = lax.optimization_barrier(jnp.sum(residual * residual, axis=0))
    for step in range(ITERS):
        applied = apply_operator(direction, graph_tiles, tile_column, live_slot)
        step_size = norm_now / lax.optimization_barrier(jnp.sum(direction * applied, axis=0))
        solution = solution + step_size[None, :] * direction
        residual = residual - step_size[None, :] * applied
        norm_next = lax.optimization_barrier(jnp.sum(residual * residual, axis=0))
        direction = residual + (norm_next / norm_now)[None, :] * direction
        norm_now = norm_next
    length = jnp.sqrt(lax.optimization_barrier(jnp.sum(solution * solution, axis=1, keepdims=True)) + 1e-06)
    return (solution / length, residual)
```

```python
import functools
import jax
import jax.numpy as jnp
from jax import lax
from jax.experimental import pallas as pl
from jax.experimental.pallas import tpu as pltpu
from jax.sharding import PartitionSpec as P

ITERS = 3


damping = 0.99
smoothing = 0.1


def edges(cells, width):
    count = lax.axis_size("rows")
    ahead = [(i, (i + 1) % count) for i in range(count)]
    behind = [((i + 1) % count, i) for i in range(count)]
    left = lax.ppermute(cells[-width:], "rows", ahead)
    right = lax.ppermute(cells[:width], "rows", behind)
    return jnp.concatenate([left, cells, right], axis=0)


def product_kernel(index_ref, count_ref, tiles_ref, blocks_ref, direction_ref, residual_ref, image_ref, dots_ref):
    row = pl.program_id(0)
    slots = tiles_ref.shape[1]
    live = count_ref[row]
    lhs = jnp.concatenate([tiles_ref[0, k] for k in range(slots)], axis=1)
    picked = []
    for k in range(slots):
        block = blocks_ref[index_ref[row, k]]
        picked.append(jnp.where(k < live, block, jnp.zeros_like(block)))
    rhs = jnp.concatenate(picked, axis=0)
    total = jnp.dot(lhs, rhs, preferred_element_type=jnp.float32)
    direction = direction_ref[0]
    residual = residual_ref[0]
    image = direction - damping * total
    image_ref[0] = image

    @pl.when(row == 0)
    def _():
        dots_ref[...] = jnp.zeros_like(dots_ref)

    def add(at, value):
        dots_ref[at : at + 1] += jnp.sum(value, axis=0, keepdims=True)

    add(0, direction * image)
    add(1, residual * image)
    add(2, image * image)
    add(3, residual * residual)


def product(index, count, tiles, blocks, direction, residual):
    rows, slots, size, _ = tiles.shape
    span, _, classes = blocks.shape
    by_row = pl.BlockSpec((1, size, classes), lambda i, a, b: (i, 0, 0))
    return pl.pallas_call(
        product_kernel,
        grid_spec=pltpu.PrefetchScalarGridSpec(
            num_scalar_prefetch=2,
            grid=(rows,),
            in_specs=[
                pl.BlockSpec((1, slots, size, size), lambda i, a, b: (i, 0, 0, 0)),
                pl.BlockSpec((span, size, classes), lambda i, a, b: (0, 0, 0)),
                by_row,
                by_row,
            ],
            out_specs=[by_row, pl.BlockSpec((8, classes), lambda i, a, b: (0, 0))],
        ),
        out_shape=[
            jax.ShapeDtypeStruct((rows, size, classes), jnp.float32),
            jax.ShapeDtypeStruct((8, classes), jnp.float32),
        ],
        compiler_params=pltpu.CompilerParams(vmem_limit_bytes=32 * 2**20),
    )(index, count, tiles, blocks, direction, residual)


def body(graph_tiles, tile_column, tile_count, class_label, confidence, class_weight):
    block_rows, slot_count, block_size, _ = graph_tiles.shape
    class_dev = class_weight.shape[0]
    half_span = block_rows // 2
    total_blocks = block_rows * lax.axis_size("rows")
    first_row = lax.axis_index("rows") * block_rows - half_span
    index = jnp.mod(tile_column - first_row, total_blocks)
    index = jnp.minimum(index, block_rows + 2 * half_span - 1)
    class_ids = lax.axis_index("cols") * class_dev + jnp.arange(class_dev, dtype=jnp.int32)
    width = half_span * block_size
    labels = edges(class_label, width).reshape(-1, block_size, 1)
    weights = edges(confidence, width).reshape(-1, block_size, 1)
    onehot = (labels == class_ids).astype(jnp.float32)
    prior = (
        weights
        * class_weight
        * ((1.0 - smoothing) * onehot + smoothing / (class_dev * lax.axis_size("cols")))
    )
    residual = direction = prior[half_span:-half_span]
    half = prior.astype(jnp.bfloat16)
    solved = 0.0
    for step in range(ITERS):
        if step:
            half = edges(direction.astype(jnp.bfloat16), half_span)
        image, dots = product(index, tile_count, graph_tiles, half, direction, residual)
        dots = lax.psum(dots, "rows")
        if step == 0:
            norm_now = dots[3]
        step_size = norm_now / dots[0]
        solved = solved + step_size * direction
        residual = residual - step_size * image
        if step < ITERS - 1:
            norm_next = norm_now + step_size * (step_size * dots[2] - 2.0 * dots[1])
            norm_next = jnp.maximum(norm_next, 0.0)
            direction = residual + (norm_next / norm_now) * direction
            norm_now = norm_next
    row_squares = lax.psum(jnp.sum(solved * solved, axis=2), "cols")
    length = jnp.sqrt(row_squares + 1e-06)
    flat = (block_rows * block_size, class_dev)
    return ((solved / length[:, :, None]).reshape(flat), residual.reshape(flat))


def solution(mesh):
    placed = (
        P("rows", None, None, None),
        P("rows", None),
        P("rows"),
        P("rows"),
        P("rows"),
        P("cols"),
    )
    return jax.shard_map(
        body,
        mesh=mesh,
        in_specs=placed,
        out_specs=(P("rows", "cols"), P("rows", "cols")),
        check_vma=False,
    )
```

```python
import functools
import jax
import jax.numpy as jnp
from jax import lax
from jax.experimental import pallas as pl
from jax.experimental.pallas import tpu as pltpu
from jax.sharding import PartitionSpec as P

ITERS = 3


damping = 0.99
smoothing = 0.1


def edges(cells, width):
    count = lax.axis_size("rows")
    ahead = [(i, (i + 1) % count) for i in range(count)]
    behind = [((i + 1) % count, i) for i in range(count)]
    left = lax.ppermute(cells[-width:], "rows", ahead)
    right = lax.ppermute(cells[:width], "rows", behind)
    return jnp.concatenate([left, cells, right], axis=0)


def product_kernel(index_ref, count_ref, tiles_ref, blocks_ref, direction_ref, residual_ref, image_ref, dots_ref):
    row = pl.program_id(0)
    slots = tiles_ref.shape[1]
    live = count_ref[row]
    lhs = jnp.concatenate([tiles_ref[0, k] for k in range(slots)], axis=1)
    picked = []
    for k in range(slots):
        block = blocks_ref[index_ref[row, k]]
        picked.append(jnp.where(k < live, block, jnp.zeros_like(block)))
    rhs = jnp.concatenate(picked, axis=0)
    total = jnp.dot(lhs, rhs, preferred_element_type=jnp.float32)
    direction = direction_ref[0]
    residual = residual_ref[0]
    image = direction - damping * total
    image_ref[0] = image

    @pl.when(row == 0)
    def _():
        dots_ref[...] = jnp.zeros_like(dots_ref)

    classes = image.shape[1]

    def column(value):
        return jnp.sum(value, axis=0, keepdims=True)

    def held(at):
        return dots_ref[at : at + 1, 0:classes]

    weight = column(image * image)
    best = column(residual * image) / jnp.where(weight > 0, weight, 1.0)
    rest = residual - best * image
    low = column(rest * rest)
    mean, mass, least = held(1), held(2), held(4)
    total_mass = mass + weight
    share = weight / jnp.where(total_mass > 0, total_mass, 1.0)
    gap = best - mean
    dots_ref[0:1, 0:classes] = held(0) + column(direction * image)
    dots_ref[1:2, 0:classes] = mean + gap * share
    dots_ref[2:3, 0:classes] = total_mass
    dots_ref[3:4, 0:classes] = held(3) + column(residual * residual)
    dots_ref[4:5, 0:classes] = least + low + gap * gap * (mass * share)


def product(index, count, tiles, blocks, direction, residual):
    rows, slots, size, _ = tiles.shape
    span, _, classes = blocks.shape
    lanes = pl.cdiv(classes, 128) * 128
    by_row = pl.BlockSpec((1, size, classes), lambda i, a, b: (i, 0, 0))
    return pl.pallas_call(
        product_kernel,
        grid_spec=pltpu.PrefetchScalarGridSpec(
            num_scalar_prefetch=2,
            grid=(rows,),
            in_specs=[
                pl.BlockSpec((1, slots, size, size), lambda i, a, b: (i, 0, 0, 0)),
                pl.BlockSpec((span, size, classes), lambda i, a, b: (0, 0, 0)),
                by_row,
                by_row,
            ],
            out_specs=[by_row, pl.BlockSpec((8, lanes), lambda i, a, b: (0, 0))],
        ),
        out_shape=[
            jax.ShapeDtypeStruct((rows, size, classes), jnp.float32),
            jax.ShapeDtypeStruct((8, lanes), jnp.float32),
        ],
        compiler_params=pltpu.CompilerParams(vmem_limit_bytes=32 * 2**20),
    )(index, count, tiles, blocks, direction, residual)


def gather_kernel(axis, count, part_ref, all_ref, send_sem, recv_sem):
    me = lax.axis_index(axis)
    barrier = pltpu.get_barrier_semaphore()
    for ahead in range(1, count):
        peer = lax.rem(me + ahead, count)
        pl.semaphore_signal(
            barrier, inc=1, device_id={axis: peer}, device_id_type=pl.DeviceIdType.MESH
        )
    pl.semaphore_wait(barrier, count - 1)
    copies = []
    for ahead in range(1, count):
        peer = lax.rem(me + ahead, count)
        copy = pltpu.make_async_remote_copy(
            src_ref=part_ref,
            dst_ref=all_ref.at[me],
            send_sem=send_sem.at[ahead],
            recv_sem=recv_sem.at[ahead],
            device_id={axis: peer},
            device_id_type=pl.DeviceIdType.MESH,
        )
        copy.start()
        copies.append(copy)
    all_ref[me] = part_ref[...]
    for copy in copies:
        copy.wait()


def gathered(part, axis, collective_id):
    count = lax.axis_size(axis)
    return pl.pallas_call(
        functools.partial(gather_kernel, axis, count),
        out_shape=jax.ShapeDtypeStruct((count,) + part.shape, part.dtype),
        in_specs=[pl.BlockSpec(memory_space=pltpu.VMEM)],
        out_specs=pl.BlockSpec(memory_space=pltpu.VMEM),
        scratch_shapes=[pltpu.SemaphoreType.DMA((count,)), pltpu.SemaphoreType.DMA((count,))],
        compiler_params=pltpu.CompilerParams(
            collective_id=collective_id, has_side_effects=True
        ),
    )(part)


def body(graph_tiles, tile_column, tile_count, class_label, confidence, class_weight):
    block_rows, slot_count, block_size, _ = graph_tiles.shape
    class_dev = class_weight.shape[0]
    half_span = block_rows // 2
    total_blocks = block_rows * lax.axis_size("rows")
    first_row = lax.axis_index("rows") * block_rows - half_span
    index = jnp.mod(tile_column - first_row, total_blocks)
    index = jnp.minimum(index, block_rows + 2 * half_span - 1)
    class_ids = lax.axis_index("cols") * class_dev + jnp.arange(class_dev, dtype=jnp.int32)
    width = half_span * block_size
    labels = edges(class_label, width).reshape(-1, block_size, 1)
    weights = edges(confidence, width).reshape(-1, block_size, 1)
    onehot = (labels == class_ids).astype(jnp.float32)
    prior = (
        weights
        * class_weight
        * ((1.0 - smoothing) * onehot + smoothing / (class_dev * lax.axis_size("cols")))
    )
    residual = direction = prior[half_span:-half_span]
    half = prior.astype(jnp.bfloat16)
    solved = 0.0
    for step in range(ITERS):
        if step:
            half = edges(direction.astype(jnp.bfloat16), half_span)
        image, dots = product(index, tile_count, graph_tiles, half, direction, residual)
        parts = gathered(dots, "rows", 0)[:, :, :class_dev]
        curve_sum = jnp.sum(parts[:, 0], axis=0)
        if step == 0:
            norm_now = jnp.sum(parts[:, 3], axis=0)
        step_size = norm_now / curve_sum
        solved = solved + step_size * direction
        residual = residual - step_size * image
        if step < ITERS - 1:
            aside = parts[:, 1] - step_size
            norm_next = jnp.sum(parts[:, 4] + aside * aside * parts[:, 2], axis=0)
            direction = residual + (norm_next / norm_now) * direction
            norm_now = norm_next
    row_squares = jnp.sum(gathered(jnp.sum(solved * solved, axis=2), "cols", 1), axis=0)
    length = jnp.sqrt(row_squares + 1e-06)
    flat = (block_rows * block_size, class_dev)
    return ((solved / length[:, :, None]).reshape(flat), residual.reshape(flat))


def solution(mesh):
    placed = (
        P("rows", None, None, None),
        P("rows", None),
        P("rows"),
        P("rows"),
        P("rows"),
        P("cols"),
    )
    return jax.shard_map(
        body,
        mesh=mesh,
        in_specs=placed,
        out_specs=(P("rows", "cols"), P("rows", "cols")),
        check_vma=False,
    )
```

```python
import functools
import jax
import jax.numpy as jnp
from jax import lax
from jax.experimental import pallas as pl
from jax.experimental.pallas import tpu as pltpu
from jax.sharding import PartitionSpec as P

ITERS = 3


damping = 0.99
smoothing = 0.1


def edges_kernel(width, count, cells_ref, wide_ref, send_sem, recv_sem):
    me = lax.axis_index("rows")
    right = lax.rem(me + 1, count)
    left = lax.rem(me + count - 1, count)
    own = cells_ref.shape[0]
    barrier = pltpu.get_barrier_semaphore()
    for peer in (left, right):
        pl.semaphore_signal(
            barrier, inc=1, device_id={"rows": peer}, device_id_type=pl.DeviceIdType.MESH
        )
    pl.semaphore_wait(barrier, 2)
    copies = []
    for at, (peer, source, target) in enumerate(
        ((right, own - width, 0), (left, 0, own + width))
    ):
        copy = pltpu.make_async_remote_copy(
            src_ref=cells_ref.at[pl.ds(source, width)],
            dst_ref=wide_ref.at[pl.ds(target, width)],
            send_sem=send_sem.at[at],
            recv_sem=recv_sem.at[at],
            device_id={"rows": peer},
            device_id_type=pl.DeviceIdType.MESH,
        )
        copy.start()
        copies.append(copy)

    @pl.loop(0, own)
    def _(block):
        wide_ref[width + block] = cells_ref[block]

    for copy in copies:
        copy.wait()


def edges(cells, width, collective_id):
    return pl.pallas_call(
        functools.partial(edges_kernel, width, lax.axis_size("rows")),
        out_shape=jax.ShapeDtypeStruct(
            (cells.shape[0] + 2 * width,) + cells.shape[1:], cells.dtype
        ),
        in_specs=[pl.BlockSpec(memory_space=pltpu.VMEM)],
        out_specs=pl.BlockSpec(memory_space=pltpu.VMEM),
        scratch_shapes=[pltpu.SemaphoreType.DMA((2,)), pltpu.SemaphoreType.DMA((2,))],
        compiler_params=pltpu.CompilerParams(
            collective_id=collective_id, has_side_effects=True, vmem_limit_bytes=16 * 2**20
        ),
    )(cells)


def product_kernel(index_ref, count_ref, tiles_ref, blocks_ref, direction_ref, residual_ref, image_ref, dots_ref):
    row = pl.program_id(0)
    slots = tiles_ref.shape[1]
    live = count_ref[row]
    lhs = jnp.concatenate([tiles_ref[0, k] for k in range(slots)], axis=1)
    picked = []
    for k in range(slots):
        block = blocks_ref[index_ref[row, k]]
        picked.append(jnp.where(k < live, block, jnp.zeros_like(block)))
    rhs = jnp.concatenate(picked, axis=0)
    total = jnp.dot(lhs, rhs, preferred_element_type=jnp.float32)
    direction = direction_ref[0]
    residual = residual_ref[0]
    image = direction - damping * total
    image_ref[0] = image

    @pl.when(row == 0)
    def _():
        dots_ref[...] = jnp.zeros_like(dots_ref)

    classes = image.shape[1]

    def column(value):
        return jnp.sum(value, axis=0, keepdims=True)

    def held(at):
        return dots_ref[at : at + 1, 0:classes]

    weight = column(image * image)
    best = column(residual * image) / jnp.where(weight > 0, weight, 1.0)
    rest = residual - best * image
    low = column(rest * rest)
    mean, mass, least = held(1), held(2), held(4)
    total_mass = mass + weight
    share = weight / jnp.where(total_mass > 0, total_mass, 1.0)
    gap = best - mean
    dots_ref[0:1, 0:classes] = held(0) + column(direction * image)
    dots_ref[1:2, 0:classes] = mean + gap * share
    dots_ref[2:3, 0:classes] = total_mass
    dots_ref[3:4, 0:classes] = held(3) + column(residual * residual)
    dots_ref[4:5, 0:classes] = least + low + gap * gap * (mass * share)


def product(index, count, tiles, blocks, direction, residual):
    rows, slots, size, _ = tiles.shape
    span, _, classes = blocks.shape
    lanes = pl.cdiv(classes, 128) * 128
    by_row = pl.BlockSpec((1, size, classes), lambda i, a, b: (i, 0, 0))
    return pl.pallas_call(
        product_kernel,
        grid_spec=pltpu.PrefetchScalarGridSpec(
            num_scalar_prefetch=2,
            grid=(rows,),
            in_specs=[
                pl.BlockSpec((1, slots, size, size), lambda i, a, b: (i, 0, 0, 0)),
                pl.BlockSpec((span, size, classes), lambda i, a, b: (0, 0, 0)),
                by_row,
                by_row,
            ],
            out_specs=[by_row, pl.BlockSpec((8, lanes), lambda i, a, b: (0, 0))],
        ),
        out_shape=[
            jax.ShapeDtypeStruct((rows, size, classes), jnp.float32),
            jax.ShapeDtypeStruct((8, lanes), jnp.float32),
        ],
        compiler_params=pltpu.CompilerParams(vmem_limit_bytes=32 * 2**20),
    )(index, count, tiles, blocks, direction, residual)


def gather_kernel(axis, count, part_ref, all_ref, send_sem, recv_sem):
    me = lax.axis_index(axis)
    barrier = pltpu.get_barrier_semaphore()
    for ahead in range(1, count):
        peer = lax.rem(me + ahead, count)
        pl.semaphore_signal(
            barrier, inc=1, device_id={axis: peer}, device_id_type=pl.DeviceIdType.MESH
        )
    pl.semaphore_wait(barrier, count - 1)
    copies = []
    for ahead in range(1, count):
        peer = lax.rem(me + ahead, count)
        copy = pltpu.make_async_remote_copy(
            src_ref=part_ref,
            dst_ref=all_ref.at[me],
            send_sem=send_sem.at[ahead],
            recv_sem=recv_sem.at[ahead],
            device_id={axis: peer},
            device_id_type=pl.DeviceIdType.MESH,
        )
        copy.start()
        copies.append(copy)
    all_ref[me] = part_ref[...]
    for copy in copies:
        copy.wait()


def gathered(part, axis, collective_id):
    count = lax.axis_size(axis)
    return pl.pallas_call(
        functools.partial(gather_kernel, axis, count),
        out_shape=jax.ShapeDtypeStruct((count,) + part.shape, part.dtype),
        in_specs=[pl.BlockSpec(memory_space=pltpu.VMEM)],
        out_specs=pl.BlockSpec(memory_space=pltpu.VMEM),
        scratch_shapes=[pltpu.SemaphoreType.DMA((count,)), pltpu.SemaphoreType.DMA((count,))],
        compiler_params=pltpu.CompilerParams(
            collective_id=collective_id, has_side_effects=True
        ),
    )(part)


def body(graph_tiles, tile_column, tile_count, class_label, confidence, class_weight):
    block_rows, slot_count, block_size, _ = graph_tiles.shape
    class_dev = class_weight.shape[0]
    half_span = block_rows // 2
    total_blocks = block_rows * lax.axis_size("rows")
    first_row = lax.axis_index("rows") * block_rows - half_span
    index = jnp.mod(tile_column - first_row, total_blocks)
    index = jnp.minimum(index, block_rows + 2 * half_span - 1)
    class_ids = lax.axis_index("cols") * class_dev + jnp.arange(class_dev, dtype=jnp.int32)
    given = jnp.stack(
        [
            class_label.astype(jnp.float32).reshape(block_rows, block_size),
            confidence.reshape(block_rows, block_size),
        ],
        axis=1,
    )
    given = edges(given, half_span, 2)
    labels = given[:, 0, :, None]
    weights = given[:, 1, :, None]
    onehot = (labels == class_ids.astype(jnp.float32)).astype(jnp.float32)
    prior = (
        weights
        * class_weight
        * ((1.0 - smoothing) * onehot + smoothing / (class_dev * lax.axis_size("cols")))
    )
    residual = direction = prior[half_span:-half_span]
    half = prior.astype(jnp.bfloat16)
    solved = 0.0
    for step in range(ITERS):
        if step:
            half = edges(direction.astype(jnp.bfloat16), half_span, 3)
        image, dots = product(index, tile_count, graph_tiles, half, direction, residual)
        parts = gathered(dots, "rows", 0)[:, :, :class_dev]
        curve_sum = jnp.sum(parts[:, 0], axis=0)
        if step == 0:
            norm_now = jnp.sum(parts[:, 3], axis=0)
        step_size = norm_now / curve_sum
        solved = solved + step_size * direction
        residual = residual - step_size * image
        if step < ITERS - 1:
            aside = parts[:, 1] - step_size
            norm_next = jnp.sum(parts[:, 4] + aside * aside * parts[:, 2], axis=0)
            direction = residual + (norm_next / norm_now) * direction
            norm_now = norm_next
    row_squares = jnp.sum(gathered(jnp.sum(solved * solved, axis=2), "cols", 1), axis=0)
    length = jnp.sqrt(row_squares + 1e-06)
    flat = (block_rows * block_size, class_dev)
    return ((solved / length[:, :, None]).reshape(flat), residual.reshape(flat))


def solution(mesh):
    placed = (
        P("rows", None, None, None),
        P("rows", None),
        P("rows"),
        P("rows"),
        P("rows"),
        P("cols"),
    )
    return jax.shard_map(
        body,
        mesh=mesh,
        in_specs=placed,
        out_specs=(P("rows", "cols"), P("rows", "cols")),
        check_vma=False,
    )
```

```python
import functools
import jax
import jax.numpy as jnp
from jax import lax
from jax.experimental import pallas as pl
from jax.experimental.pallas import tpu as pltpu
from jax.sharding import PartitionSpec as P

ITERS = 3


damping = 0.99
smoothing = 0.1


def edges_kernel(width, count, cells_ref, wide_ref, send_sem, recv_sem):
    me = lax.axis_index("rows")
    right = lax.rem(me + 1, count)
    left = lax.rem(me + count - 1, count)
    own = cells_ref.shape[0]
    barrier = pltpu.get_barrier_semaphore()
    for peer in (left, right):
        pl.semaphore_signal(
            barrier, inc=1, device_id={"rows": peer}, device_id_type=pl.DeviceIdType.MESH
        )
    pl.semaphore_wait(barrier, 2)
    copies = []
    for at, (peer, source, target) in enumerate(
        ((right, own - width, 0), (left, 0, own + width))
    ):
        copy = pltpu.make_async_remote_copy(
            src_ref=cells_ref.at[pl.ds(source, width)],
            dst_ref=wide_ref.at[pl.ds(target, width)],
            send_sem=send_sem.at[at],
            recv_sem=recv_sem.at[at],
            device_id={"rows": peer},
            device_id_type=pl.DeviceIdType.MESH,
        )
        copy.start()
        copies.append(copy)

    @pl.loop(0, own)
    def _(block):
        wide_ref[width + block] = cells_ref[block]

    for copy in copies:
        copy.wait()


def edges(cells, width, collective_id):
    return pl.pallas_call(
        functools.partial(edges_kernel, width, lax.axis_size("rows")),
        out_shape=jax.ShapeDtypeStruct(
            (cells.shape[0] + 2 * width,) + cells.shape[1:], cells.dtype
        ),
        in_specs=[pl.BlockSpec(memory_space=pltpu.VMEM)],
        out_specs=pl.BlockSpec(memory_space=pltpu.VMEM),
        scratch_shapes=[pltpu.SemaphoreType.DMA((2,)), pltpu.SemaphoreType.DMA((2,))],
        compiler_params=pltpu.CompilerParams(
            collective_id=collective_id, has_side_effects=True, vmem_limit_bytes=8 * 2**20
        ),
    )(cells)


def product_kernel(index_ref, count_ref, tiles_ref, blocks_ref, direction_ref, residual_ref, image_ref, dots_ref):
    row = pl.program_id(0)
    slots = tiles_ref.shape[1]
    live = count_ref[row]
    lhs = jnp.concatenate([tiles_ref[0, k] for k in range(slots)], axis=1)
    picked = []
    for k in range(slots):
        block = blocks_ref[index_ref[row, k]]
        picked.append(jnp.where(k < live, block, jnp.zeros_like(block)))
    rhs = jnp.concatenate(picked, axis=0)
    total = jnp.dot(lhs, rhs, preferred_element_type=jnp.float32)
    direction = direction_ref[0]
    residual = residual_ref[0]
    image = direction - damping * total
    image_ref[0] = image

    @pl.when(row == 0)
    def _():
        dots_ref[...] = jnp.zeros_like(dots_ref)

    classes = image.shape[1]

    def column(value):
        return jnp.sum(value, axis=0, keepdims=True)

    def held(at):
        return dots_ref[at : at + 1, 0:classes]

    weight = column(image * image)
    best = column(residual * image) / jnp.where(weight > 0, weight, 1.0)
    rest = residual - best * image
    low = column(rest * rest)
    mean, mass, least = held(1), held(2), held(4)
    total_mass = mass + weight
    share = weight / jnp.where(total_mass > 0, total_mass, 1.0)
    gap = best - mean
    dots_ref[0:1, 0:classes] = held(0) + column(direction * image)
    dots_ref[1:2, 0:classes] = mean + gap * share
    dots_ref[2:3, 0:classes] = total_mass
    dots_ref[3:4, 0:classes] = held(3) + column(residual * residual)
    dots_ref[4:5, 0:classes] = least + low + gap * gap * (mass * share)


def product(index, count, tiles, blocks, direction, residual):
    rows, slots, size, _ = tiles.shape
    span, _, classes = blocks.shape
    lanes = pl.cdiv(classes, 128) * 128
    by_row = pl.BlockSpec((1, size, classes), lambda i, a, b: (i, 0, 0))
    return pl.pallas_call(
        product_kernel,
        grid_spec=pltpu.PrefetchScalarGridSpec(
            num_scalar_prefetch=2,
            grid=(rows,),
            in_specs=[
                pl.BlockSpec((1, slots, size, size), lambda i, a, b: (i, 0, 0, 0)),
                pl.BlockSpec((span, size, classes), lambda i, a, b: (0, 0, 0)),
                by_row,
                by_row,
            ],
            out_specs=[by_row, pl.BlockSpec((8, lanes), lambda i, a, b: (0, 0))],
        ),
        out_shape=[
            jax.ShapeDtypeStruct((rows, size, classes), jnp.float32),
            jax.ShapeDtypeStruct((8, lanes), jnp.float32),
        ],
        compiler_params=pltpu.CompilerParams(vmem_limit_bytes=16 * 2**20),
    )(index, count, tiles, blocks, direction, residual)


def gather_kernel(axis, count, part_ref, all_ref, send_sem, recv_sem):
    me = lax.axis_index(axis)
    barrier = pltpu.get_barrier_semaphore()
    for ahead in range(1, count):
        peer = lax.rem(me + ahead, count)
        pl.semaphore_signal(
            barrier, inc=1, device_id={axis: peer}, device_id_type=pl.DeviceIdType.MESH
        )
    pl.semaphore_wait(barrier, count - 1)
    copies = []
    for ahead in range(1, count):
        peer = lax.rem(me + ahead, count)
        copy = pltpu.make_async_remote_copy(
            src_ref=part_ref,
            dst_ref=all_ref.at[me],
            send_sem=send_sem.at[ahead],
            recv_sem=recv_sem.at[ahead],
            device_id={axis: peer},
            device_id_type=pl.DeviceIdType.MESH,
        )
        copy.start()
        copies.append(copy)
    all_ref[me] = part_ref[...]
    for copy in copies:
        copy.wait()


def gathered(part, axis, collective_id):
    count = lax.axis_size(axis)
    return pl.pallas_call(
        functools.partial(gather_kernel, axis, count),
        out_shape=jax.ShapeDtypeStruct((count,) + part.shape, part.dtype),
        in_specs=[pl.BlockSpec(memory_space=pltpu.VMEM)],
        out_specs=pl.BlockSpec(memory_space=pltpu.VMEM),
        scratch_shapes=[pltpu.SemaphoreType.DMA((count,)), pltpu.SemaphoreType.DMA((count,))],
        compiler_params=pltpu.CompilerParams(
            collective_id=collective_id, has_side_effects=True, vmem_limit_bytes=2 * 2**20
        ),
    )(part)


def body(graph_tiles, tile_column, tile_count, class_label, confidence, class_weight):
    block_rows, slot_count, block_size, _ = graph_tiles.shape
    class_dev = class_weight.shape[0]
    half_span = block_rows // 2
    total_blocks = block_rows * lax.axis_size("rows")
    first_row = lax.axis_index("rows") * block_rows - half_span
    index = jnp.mod(tile_column - first_row, total_blocks)
    index = jnp.minimum(index, block_rows + 2 * half_span - 1)
    class_ids = lax.axis_index("cols") * class_dev + jnp.arange(class_dev, dtype=jnp.int32)
    given = jnp.stack(
        [
            class_label.astype(jnp.float32).reshape(block_rows, block_size),
            confidence.reshape(block_rows, block_size),
        ],
        axis=1,
    )
    given = edges(given, half_span, 2)
    labels = given[:, 0, :, None]
    weights = given[:, 1, :, None]
    onehot = (labels == class_ids.astype(jnp.float32)).astype(jnp.float32)
    prior = (
        weights
        * class_weight
        * ((1.0 - smoothing) * onehot + smoothing / (class_dev * lax.axis_size("cols")))
    )
    residual = direction = prior[half_span:-half_span]
    half = prior.astype(jnp.bfloat16)
    solved = 0.0
    for step in range(ITERS):
        if step:
            half = edges(direction.astype(jnp.bfloat16), half_span, 3)
        image, dots = product(index, tile_count, graph_tiles, half, direction, residual)
        parts = gathered(dots, "rows", 0)[:, :, :class_dev]
        curve_sum = jnp.sum(parts[:, 0], axis=0)
        if step == 0:
            norm_now = jnp.sum(parts[:, 3], axis=0)
        step_size = norm_now / curve_sum
        solved = solved + step_size * direction
        residual = residual - step_size * image
        if step < ITERS - 1:
            aside = parts[:, 1] - step_size
            norm_next = jnp.sum(parts[:, 4] + aside * aside * parts[:, 2], axis=0)
            direction = residual + (norm_next / norm_now) * direction
            norm_now = norm_next
    row_squares = jnp.sum(gathered(jnp.sum(solved * solved, axis=2), "cols", 1), axis=0)
    length = jnp.sqrt(row_squares + 1e-06)
    flat = (block_rows * block_size, class_dev)
    return ((solved / length[:, :, None]).reshape(flat), residual.reshape(flat))


def solution(mesh):
    placed = (
        P("rows", None, None, None),
        P("rows", None),
        P("rows"),
        P("rows"),
        P("rows"),
        P("cols"),
    )
    return jax.shard_map(
        body,
        mesh=mesh,
        in_specs=placed,
        out_specs=(P("rows", "cols"), P("rows", "cols")),
        check_vma=False,
    )
```

```python
import functools
import jax
import jax.numpy as jnp
from jax import lax
from jax.experimental import pallas as pl
from jax.experimental.pallas import tpu as pltpu
from jax.sharding import PartitionSpec as P

ITERS = 3


damping = 0.99
smoothing = 0.1


def edges_kernel(width, count, cells_ref, wide_ref, send_sem, recv_sem):
    me = lax.axis_index("rows")
    right = lax.rem(me + 1, count)
    left = lax.rem(me + count - 1, count)
    own = cells_ref.shape[0]
    barrier = pltpu.get_barrier_semaphore()
    for peer in (left, right):
        pl.semaphore_signal(
            barrier, inc=1, device_id={"rows": peer}, device_id_type=pl.DeviceIdType.MESH
        )
    pl.semaphore_wait(barrier, 2)
    copies = []
    for at, (peer, source, target) in enumerate(
        ((right, own - width, 0), (left, 0, own + width))
    ):
        copy = pltpu.make_async_remote_copy(
            src_ref=cells_ref.at[pl.ds(source, width)],
            dst_ref=wide_ref.at[pl.ds(target, width)],
            send_sem=send_sem.at[at],
            recv_sem=recv_sem.at[at],
            device_id={"rows": peer},
            device_id_type=pl.DeviceIdType.MESH,
        )
        copy.start()
        copies.append(copy)

    @pl.loop(0, own)
    def _(block):
        wide_ref[width + block] = cells_ref[block]

    for copy in copies:
        copy.wait()


def edges(cells, width, collective_id):
    return pl.pallas_call(
        functools.partial(edges_kernel, width, lax.axis_size("rows")),
        out_shape=jax.ShapeDtypeStruct(
            (cells.shape[0] + 2 * width,) + cells.shape[1:], cells.dtype
        ),
        in_specs=[pl.BlockSpec(memory_space=pltpu.VMEM)],
        out_specs=pl.BlockSpec(memory_space=pltpu.VMEM),
        scratch_shapes=[pltpu.SemaphoreType.DMA((2,)), pltpu.SemaphoreType.DMA((2,))],
        compiler_params=pltpu.CompilerParams(
            collective_id=collective_id, has_side_effects=True, vmem_limit_bytes=8 * 2**20
        ),
    )(cells)


def product_kernel(index_ref, count_ref, tiles_ref, blocks_ref, direction_ref, residual_ref, image_ref, dots_ref):
    together = tiles_ref.shape[0]
    first = pl.program_id(0) * together
    slots = tiles_ref.shape[1]

    @pl.when(first == 0)
    def _():
        dots_ref[...] = jnp.zeros_like(dots_ref)

    for at in range(together):
        row = first + at
        live = count_ref[row]
        lhs = jnp.concatenate([tiles_ref[at, k] for k in range(slots)], axis=1)
        picked = []
        for k in range(slots):
            block = blocks_ref[index_ref[row, k]]
            picked.append(jnp.where(k < live, block, jnp.zeros_like(block)))
        rhs = jnp.concatenate(picked, axis=0)
        total = jnp.dot(lhs, rhs, preferred_element_type=jnp.float32)
        direction = direction_ref[at]
        residual = residual_ref[at]
        image = direction - damping * total
        image_ref[at] = image

        classes = image.shape[1]

        def column(value):
            return jnp.sum(value, axis=0, keepdims=True)

        def held(line):
            return dots_ref[line : line + 1, 0:classes]

        weight = column(image * image)
        best = column(residual * image) / jnp.where(weight > 0, weight, 1.0)
        rest = residual - best * image
        low = column(rest * rest)
        mean, mass, least = held(1), held(2), held(4)
        total_mass = mass + weight
        share = weight / jnp.where(total_mass > 0, total_mass, 1.0)
        gap = best - mean
        dots_ref[0:1, 0:classes] = held(0) + column(direction * image)
        dots_ref[1:2, 0:classes] = mean + gap * share
        dots_ref[2:3, 0:classes] = total_mass
        dots_ref[3:4, 0:classes] = held(3) + column(residual * residual)
        dots_ref[4:5, 0:classes] = least + low + gap * gap * (mass * share)


def product(index, count, tiles, blocks, direction, residual):
    rows, slots, size, _ = tiles.shape
    span, _, classes = blocks.shape
    lanes = pl.cdiv(classes, 128) * 128
    together = 2 if rows % 2 == 0 else 1
    by_row = pl.BlockSpec((together, size, classes), lambda i, a, b: (i, 0, 0))
    return pl.pallas_call(
        product_kernel,
        grid_spec=pltpu.PrefetchScalarGridSpec(
            num_scalar_prefetch=2,
            grid=(rows // together,),
            in_specs=[
                pl.BlockSpec((together, slots, size, size), lambda i, a, b: (i, 0, 0, 0)),
                pl.BlockSpec((span, size, classes), lambda i, a, b: (0, 0, 0)),
                by_row,
                by_row,
            ],
            out_specs=[by_row, pl.BlockSpec((8, lanes), lambda i, a, b: (0, 0))],
        ),
        out_shape=[
            jax.ShapeDtypeStruct((rows, size, classes), jnp.float32),
            jax.ShapeDtypeStruct((8, lanes), jnp.float32),
        ],
        compiler_params=pltpu.CompilerParams(vmem_limit_bytes=16 * 2**20),
    )(index, count, tiles, blocks, direction, residual)


def gather_kernel(axis, count, part_ref, all_ref, send_sem, recv_sem):
    me = lax.axis_index(axis)
    barrier = pltpu.get_barrier_semaphore()
    for ahead in range(1, count):
        peer = lax.rem(me + ahead, count)
        pl.semaphore_signal(
            barrier, inc=1, device_id={axis: peer}, device_id_type=pl.DeviceIdType.MESH
        )
    pl.semaphore_wait(barrier, count - 1)
    copies = []
    for ahead in range(1, count):
        peer = lax.rem(me + ahead, count)
        copy = pltpu.make_async_remote_copy(
            src_ref=part_ref,
            dst_ref=all_ref.at[me],
            send_sem=send_sem.at[ahead],
            recv_sem=recv_sem.at[ahead],
            device_id={axis: peer},
            device_id_type=pl.DeviceIdType.MESH,
        )
        copy.start()
        copies.append(copy)
    all_ref[me] = part_ref[...]
    for copy in copies:
        copy.wait()


def gathered(part, axis, collective_id):
    count = lax.axis_size(axis)
    return pl.pallas_call(
        functools.partial(gather_kernel, axis, count),
        out_shape=jax.ShapeDtypeStruct((count,) + part.shape, part.dtype),
        in_specs=[pl.BlockSpec(memory_space=pltpu.VMEM)],
        out_specs=pl.BlockSpec(memory_space=pltpu.VMEM),
        scratch_shapes=[pltpu.SemaphoreType.DMA((count,)), pltpu.SemaphoreType.DMA((count,))],
        compiler_params=pltpu.CompilerParams(
            collective_id=collective_id, has_side_effects=True, vmem_limit_bytes=2 * 2**20
        ),
    )(part)


def body(graph_tiles, tile_column, tile_count, class_label, confidence, class_weight):
    block_rows, slot_count, block_size, _ = graph_tiles.shape
    class_dev = class_weight.shape[0]
    half_span = block_rows // 2
    total_blocks = block_rows * lax.axis_size("rows")
    first_row = lax.axis_index("rows") * block_rows - half_span
    index = jnp.mod(tile_column - first_row, total_blocks)
    index = jnp.minimum(index, block_rows + 2 * half_span - 1)
    class_ids = lax.axis_index("cols") * class_dev + jnp.arange(class_dev, dtype=jnp.int32)
    given = jnp.stack(
        [
            class_label.astype(jnp.float32).reshape(block_rows, block_size),
            confidence.reshape(block_rows, block_size),
        ],
        axis=1,
    )
    given = edges(given, half_span, 2)
    labels = given[:, 0, :, None]
    weights = given[:, 1, :, None]
    onehot = (labels == class_ids.astype(jnp.float32)).astype(jnp.float32)
    prior = (
        weights
        * class_weight
        * ((1.0 - smoothing) * onehot + smoothing / (class_dev * lax.axis_size("cols")))
    )
    residual = direction = prior[half_span:-half_span]
    half = prior.astype(jnp.bfloat16)
    solved = 0.0
    for step in range(ITERS):
        if step:
            half = edges(direction.astype(jnp.bfloat16), half_span, 3)
        image, dots = product(index, tile_count, graph_tiles, half, direction, residual)
        parts = gathered(dots, "rows", 0)[:, :, :class_dev]
        curve_sum = jnp.sum(parts[:, 0], axis=0)
        if step == 0:
            norm_now = jnp.sum(parts[:, 3], axis=0)
        step_size = norm_now / curve_sum
        solved = solved + step_size * direction
        residual = residual - step_size * image
        if step < ITERS - 1:
            aside = parts[:, 1] - step_size
            norm_next = jnp.sum(parts[:, 4] + aside * aside * parts[:, 2], axis=0)
            direction = residual + (norm_next / norm_now) * direction
            norm_now = norm_next
    row_squares = jnp.sum(gathered(jnp.sum(solved * solved, axis=2), "cols", 1), axis=0)
    length = jnp.sqrt(row_squares + 1e-06)
    flat = (block_rows * block_size, class_dev)
    return ((solved / length[:, :, None]).reshape(flat), residual.reshape(flat))


def solution(mesh):
    placed = (
        P("rows", None, None, None),
        P("rows", None),
        P("rows"),
        P("rows"),
        P("rows"),
        P("cols"),
    )
    return jax.shard_map(
        body,
        mesh=mesh,
        in_specs=placed,
        out_specs=(P("rows", "cols"), P("rows", "cols")),
        check_vma=False,
    )
```
